512 devices in a mesh: ctx: 64 (over z, y_lo, core), head: 8 (over x, y_hi).
Axes of the slice: x: 4, y: 4 (y_hi: 2, y_lo: 2; y = y_hi * 2 + y_lo), z: 16, core: 2. Of those that a mesh axis runs over, the one named last changes fastest.
Arguments:
- embeddings: bfloat16 [16384, 8192], P('ctx', 'head'), may hold values from -6 to 6
- adapter_down: bfloat16 [8192, 8], P('head'), may hold values from -0.0625 to 0.0625
- adapter_up: bfloat16 [8, 8192], P(None, 'head'), may hold values from -0.8984375 to 0.8984375
- query_base: bfloat16 [16384, 8192], P('ctx', 'head'), may hold values from -24 to 24
- key_states: bfloat16 [16384, 1024], P('ctx', 'head'), may hold values from -24 to 24
- values: bfloat16 [16384, 1024], P('ctx', 'head'), may hold values from -6 to 6
- grad_out: bfloat16 [16384, 8192], P('ctx', 'head'), may hold values from -36 to 36
Outputs:
- attn_out: bfloat16 [16384, 8192], P('ctx', 'head')
- grad_embeddings: float32 [16384, 8192], P('ctx', 'head')
- grad_adapter_down: float32 [8192, 8], P('head')
- grad_adapter_up: float32 [8, 8192], P(None, 'head')
- grad_key_states: float32 [16384, 1024], P('ctx', 'head')
- grad_values: float32 [16384, 1024], P('ctx', 'head')
The draws below stay inside these ranges and needn't reach their ends.
All inputs are finite; a program needn't handle non-finite values.
Results may differ from the reference program's by a relative error of at most 0.0095.
The reference program's roundings to bfloat16 on the way (of `query`, `weight_b` and `dscore`) count: a program that leaves them out, or rounds other values in their place, can miss the bound.
Values may be sent and summed in bfloat16 or wider, within the bound.
No kernel may reach another device: no remote copies, remote signals or barrier semaphores. Data moves between devices by JAX's collectives and lax.ppermute only.
A program may use at most 64 MiB of HBM per device.

```python
import math
import jax
import jax.numpy as jnp
from jax import lax

D = 8192
H = 64
KVH = 8
HD = 128
R = 8
TOKENS = 16384
GROUP = 1024
SHIFT = 512


def draw_query_base(key, part):
    key = jax.random.fold_in(key, 11)
    base = jnp.clip(jax.random.normal(key, (TOKENS, H * HD), jnp.float32), -6.0, 6.0)
    return base.astype(jnp.bfloat16)


def draw_key_states(key, part):
    key = jax.random.fold_in(key, 23)
    base = jnp.clip(jax.random.normal(key, (TOKENS, KVH * HD), jnp.float32), -6.0, 6.0)
    return base.astype(jnp.bfloat16)


def draw_grad_out(key, part):
    key = jax.random.fold_in(key, 37)
    position = jnp.arange(TOKENS).astype(jnp.float32) / TOKENS
    noise = jnp.clip(jax.random.normal(key, (TOKENS, H * HD), jnp.float32), -4.0, 4.0)
    base = noise * jnp.exp(jnp.log(3.0) * position)[:, None]
    return base.astype(jnp.bfloat16)


def block_scale(stream_key, extent, shards, least, largest):
    gain, own = 1.0, jax.random.fold_in(stream_key, 6)
    for dim, blocks in shards:
        heights = jnp.exp(jax.random.uniform(jax.random.fold_in(own, dim), (blocks,), jnp.float32, least / len(shards), largest / len(shards)))
        gain = gain * jnp.repeat(heights, extent[dim] // blocks).reshape([-1 if axis == dim else 1 for axis in range(len(extent))])
    return gain


def bell_draw(rng, shape, width, reach, cuts=(), kind=jnp.bfloat16):
    array = jax.random.normal(rng, shape, jnp.float32) * width
    if len(cuts) > 0:
        array = block_scale(rng, shape, cuts, -0.22, 0.18) * array
    return jnp.clip(array, min=-reach, max=reach).astype(kind)


def setup_inputs(seed: int = 0) -> dict:
    keys = jax.random.split(jax.random.key(seed), 8)
    return {
        "embeddings": bell_draw(keys[0], (TOKENS, D), 1.0, 6.0, ((0, 64), (1, 8))),
        "adapter_down": bell_draw(keys[1], (D, R), D ** -0.5, 0.0625, ((0, 8),)),
        "adapter_up": bell_draw(keys[2], (R, H * HD), 0.15, 0.8984375, ((1, 8),)),
        "query_base": draw_query_base(jax.random.fold_in(keys[7], 71), 0),
        "key_states": draw_key_states(jax.random.fold_in(keys[7], 71), 0),
        "values": bell_draw(keys[5], (TOKENS, KVH * HD), 1.0, 6.0, ((0, 64), (1, 8))),
        "grad_out": draw_grad_out(jax.random.fold_in(keys[7], 71), 0),
    }


def group_pass(query_group, key_group, value_group, cotangent_group):
    rows = query_group.shape[0]
    inv_scale = 1.0 / math.sqrt(HD)
    query_f = query_group.astype(jnp.float32)
    key_f = key_group.astype(jnp.float32)
    value_f = value_group.astype(jnp.float32)
    cot_f = cotangent_group.astype(jnp.float32)
    scores = jnp.einsum('tqd,sd->tqs', query_f, key_f) * inv_scale
    order = jnp.arange(rows)
    allowed = (order[None, :] <= order[:, None])[:, None, :]
    scores = jnp.where(allowed, scores, -1e+30)
    top = lax.optimization_barrier(jnp.max(scores, axis=-1, keepdims=True))
    weight = jnp.exp(scores - top)
    weight = weight / lax.optimization_barrier(jnp.sum(weight, axis=-1, keepdims=True))
    weight_b = lax.optimization_barrier(weight.astype(jnp.bfloat16)).astype(jnp.float32)
    attn_full = jnp.einsum('tqs,sd->tqd', weight_b, value_f)
    delta = lax.optimization_barrier(jnp.sum(cot_f * attn_full, axis=-1, keepdims=True))
    dprob = jnp.einsum('tqd,sd->tqs', cot_f, value_f)
    dscore = lax.optimization_barrier((weight * (dprob - delta)).astype(jnp.bfloat16)).astype(jnp.float32)
    grad_q = jnp.einsum('tqs,sd->tqd', dscore, key_f) * inv_scale
    grad_k = jnp.einsum('tqs,tqd->sd', dscore, query_f) * inv_scale
    grad_v = jnp.einsum('tqs,tqd->sd', weight_b, cot_f)
    return (attn_full.astype(jnp.bfloat16), grad_q, grad_k, grad_v)

def reference(embeddings, adapter_down, adapter_up, query_base, key_states, values, grad_out):
    highest = lax.Precision.HIGHEST
    inner = jnp.dot(embeddings, adapter_down, preferred_element_type=jnp.float32)
    up_float = adapter_up.astype(jnp.float32)
    query = (query_base.astype(jnp.float32) + 2.0 * jnp.dot(inner, up_float, precision=highest)).astype(jnp.bfloat16)
    per_kv = H // KVH
    groups = TOKENS // GROUP
    query3 = query.reshape(TOKENS, H, HD)
    key3 = key_states.reshape(TOKENS, KVH, HD)
    value3 = values.reshape(TOKENS, KVH, HD)
    cot3 = grad_out.reshape(TOKENS, H, HD)
    outs, grad_qs, grad_ks, grad_vs = ([], [], [], [])
    for kv_head in range(KVH):
        arrays = [query3[:, kv_head * per_kv:(kv_head + 1) * per_kv], key3[:, kv_head], value3[:, kv_head], cot3[:, kv_head * per_kv:(kv_head + 1) * per_kv]]
        shifted = kv_head >= KVH // 2
        if shifted:
            arrays = [jnp.roll(item, -SHIFT, axis=0) for item in arrays]
        blocks = (arrays[0].reshape(groups, GROUP, per_kv, HD), arrays[1].reshape(groups, GROUP, HD), arrays[2].reshape(groups, GROUP, HD), arrays[3].reshape(groups, GROUP, per_kv, HD))
        result = lax.map(lambda items: group_pass(*items), blocks)
        pieces = [result[0].reshape(TOKENS, per_kv * HD), result[1].reshape(TOKENS, per_kv * HD), result[2].reshape(TOKENS, HD), result[3].reshape(TOKENS, HD)]
        if shifted:
            pieces = [jnp.roll(item, SHIFT, axis=0) for item in pieces]
        outs.append(pieces[0])
        grad_qs.append(pieces[1])
        grad_ks.append(pieces[2])
        grad_vs.append(pieces[3])
    attn_out = jnp.concatenate(outs, axis=1)
    grad_query = jnp.concatenate(grad_qs, axis=1)
    grad_key_states = jnp.concatenate(grad_ks, axis=1)
    grad_values = jnp.concatenate(grad_vs, axis=1)
    grad_adapter_up = 2.0 * jnp.dot(inner.T, grad_query, precision=highest)
    grad_inner = 2.0 * jnp.dot(grad_query, up_float.T, precision=highest)
    grad_adapter_down = jnp.dot(embeddings.astype(jnp.float32).T, grad_inner, precision=highest)
    grad_embeddings = jnp.dot(grad_inner, adapter_down.astype(jnp.float32).T, precision=highest)
    return (attn_out, grad_embeddings, grad_adapter_down, grad_adapter_up, grad_key_states, grad_values)
```

```python
import functools
import math

import jax
import jax.numpy as jnp
from jax import lax
from jax.experimental import pallas as pl
from jax.experimental.pallas import tpu as pltpu
from jax.sharding import PartitionSpec as P

HD = 128
SPAN = 4
FAR = 1e30
F32 = jnp.float32
BF16 = jnp.bfloat16
NT = (((1,), (1,)), ((), ()))
TN = (((0,), (0,)), ((), ()))
MAIN_VMEM = 40 * 2**20
SMALL_VMEM = 16 * 2**20


def dot(a, b, dims=(((1,), (0,)), ((), ()))):
    return lax.dot_general(a, b, dims, preferred_element_type=F32)


def split3(x):
    hi = x.astype(BF16).astype(F32)
    rest = x - hi
    mid = rest.astype(BF16).astype(F32)
    low = rest - mid
    return jnp.concatenate([hi, mid, low, jnp.zeros_like(x)], axis=0).astype(BF16)


def thrice(x):
    x = x.astype(F32)
    return jnp.concatenate([x, x, x, jnp.zeros_like(x)], axis=0).astype(BF16)


def first_kernel(emb_ref, down_ref, key_ref, value_ref, parts_ref, kv_ref):
    part = dot(down_ref[...], emb_ref[...], NT)
    for peer in range(parts_ref.shape[0]):
        parts_ref[peer] = part
    kv_ref[0] = key_ref[...]
    kv_ref[1] = value_ref[...]


def main_kernel(
    heads_per_step,
    parts_ref,
    up_ref,
    base_ref,
    cot_ref,
    own_ref,
    near_ref,
    mid_ref,
    far_ref,
    attn_ref,
    inner_parts_ref,
    part_up_ref,
    grad_own_ref,
    grad_near_ref,
    grad_mid_ref,
    grad_far_ref,
    query_ref,
    key_ref,
    value_ref,
    key_t_ref,
    value_t_ref,
    grad_q_ref,
    acc_k_ref,
    acc_v_ref,
):
    rows = base_ref.shape[0]
    heads = base_ref.shape[1] // HD
    inv_scale = 1.0 / math.sqrt(HD)
    to_exp2 = inv_scale * math.log2(math.e)
    n_head = lax.axis_size("head")
    shift = jnp.where(lax.axis_index("head") >= n_head // 2, SPAN // 2, 0)
    rank = lax.rem(lax.axis_index("ctx") + SPAN - shift, SPAN)

    inner = jnp.sum(parts_ref[...], axis=0)
    inner3 = split3(inner)
    query_ref[...] = (
        base_ref[...].astype(F32) + 2.0 * dot(inner3, thrice(up_ref[...]), TN)
    ).astype(BF16)
    for position, ref in enumerate((far_ref, mid_ref, near_ref, own_ref)):
        at = slice(position * rows, (position + 1) * rows)
        key_ref[at, :] = ref[0]
        value_ref[at, :] = ref[1]
        key_t_ref[:, at] = ref[0].astype(F32).T.astype(BF16)
        value_t_ref[:, at] = ref[1].astype(F32).T.astype(BF16)
    acc_k_ref[...] = jnp.zeros_like(acc_k_ref)
    acc_v_ref[...] = jnp.zeros_like(acc_v_ref)

    source = lax.broadcasted_iota(jnp.int32, (rows, rows), 0)
    target = lax.broadcasted_iota(jnp.int32, (rows, rows), 1)
    causal = source <= target
    closed = [jnp.where(rank >= SPAN - 1 - p, 0.0, FAR) for p in range(SPAN - 1)]

    def one_head(head):
        at = pl.ds(pl.multiple_of(head * HD, HD), HD)
        query, cot = query_ref[:, at], cot_ref[:, at]
        scores = dot(key_ref[...], query, NT)
        blocks = [scores[p * rows : (p + 1) * rows] for p in range(SPAN)]
        blocks[-1] = jnp.where(causal, blocks[-1], -FAR)
        tops = [jnp.max(block, axis=0, keepdims=True) for block in blocks]
        top = tops[-1]
        for p in range(SPAN - 1):
            top = jnp.maximum(top, tops[p] - closed[p])
        limits = [top + closed[p] for p in range(SPAN - 1)] + [top]
        powers = [jnp.exp2((b - t) * to_exp2) for b, t in zip(blocks, limits)]
        total = sum(jnp.sum(power, axis=0, keepdims=True) for power in powers)
        weight = jnp.concatenate(powers, axis=0) * (1.0 / total)
        weight_b = weight.astype(BF16)
        attn_t = dot(value_t_ref[...], weight_b)
        cot_t = cot.astype(F32).T
        delta = jnp.sum(cot_t * attn_t, axis=0, keepdims=True)
        attn_ref[:, at] = attn_t.T.astype(BF16)
        dprob = dot(value_ref[...], cot, NT)
        dscore = (weight * (dprob - delta)).astype(BF16)
        grad_q_ref[at, :] = dot(key_t_ref[...], dscore) * (2.0 * inv_scale)
        return query, cot, weight_b, dscore

    def step(i, carry):
        got = [one_head(i * heads_per_step + j) for j in range(heads_per_step)]
        query, cot = (jnp.concatenate([g[k] for g in got], axis=0) for k in (0, 1))
        weight_b, dscore = (jnp.concatenate([g[k] for g in got], axis=1) for k in (2, 3))
        acc_v_ref[...] += dot(weight_b, cot)
        acc_k_ref[...] += dot(dscore, query)
        return carry

    lax.fori_loop(0, heads // heads_per_step, step, 0)

    outs = (grad_far_ref, grad_mid_ref, grad_near_ref, grad_own_ref)
    for position, ref in enumerate(outs):
        at = slice(position * rows, (position + 1) * rows)
        ref[0] = (acc_k_ref[at, :] * inv_scale).astype(ref.dtype)
        ref[1] = acc_v_ref[at, :].astype(ref.dtype)

    grad_q = grad_q_ref[...]
    high = grad_q.astype(BF16)
    low = (grad_q - high.astype(F32)).astype(BF16)
    up = up_ref[...]
    grad_inner = dot(up, high) + dot(up, low)
    for peer in range(inner_parts_ref.shape[0]):
        inner_parts_ref[peer] = grad_inner
    r = inner.shape[0]
    rows3 = dot(inner3, high, NT)
    part_up = rows3[:r] + rows3[r : 2 * r] + rows3[2 * r : 3 * r]
    rows3 = dot(inner3, low, NT)
    part_up_ref[...] = part_up + rows3[:r] + rows3[r : 2 * r]


def last_kernel(parts_ref, emb_ref, down_ref, part_up_ref, grad_emb_ref, pieces_ref):
    grad_inner = jnp.sum(parts_ref[...], axis=0)
    r = grad_inner.shape[0]
    terms = split3(grad_inner)
    rows3 = dot(terms, emb_ref[...])
    part_down = rows3[:r] + rows3[r : 2 * r] + rows3[2 * r : 3 * r]
    grad_emb_ref[...] = dot(terms, thrice(down_ref[...]), TN)
    half = pieces_ref.shape[0] // 2
    width = pieces_ref.shape[2]
    for piece in range(half):
        at = slice(piece * width, (piece + 1) * width)
        pieces_ref[piece] = part_down[:, at]
        pieces_ref[half + piece] = part_up_ref[:, at]


def call(kernel, outs, *args, scratch=(), limit=SMALL_VMEM, name=None):
    return pl.pallas_call(
        kernel,
        out_shape=[jax.ShapeDtypeStruct(shape, dtype) for shape, dtype in outs],
        scratch_shapes=scratch,
        compiler_params=pltpu.CompilerParams(vmem_limit_bytes=limit),
        name=name,
    )(*args)


def ctx_groups(n_ctx, n_head, members):
    return [[c * n_head + h for c in group] for group in members for h in range(n_head)]


def on_device(embeddings, adapter_down, adapter_up, query_base, key_states, values, grad_out):
    rows, width = query_base.shape
    r = adapter_up.shape[0]
    n_ctx, n_head = lax.axis_size("ctx"), lax.axis_size("head")
    both = ("ctx", "head")
    keys = SPAN * rows
    down_t = adapter_down.T

    def route(distance, back=False):
        pairs = []
        for head in range(n_head):
            shift = SPAN // 2 if head >= n_head // 2 else 0
            for ctx in range(n_ctx):
                if (ctx - shift) % SPAN + distance < SPAN:
                    pair = (ctx * n_head + head, (ctx + distance) % n_ctx * n_head + head)
                    pairs.append(pair[::-1] if back else pair)
        return pairs

    parts, kv = call(
        first_kernel,
        [((n_head, r, rows), F32), ((2, rows, HD), BF16)],
        embeddings,
        down_t,
        key_states,
        values,
        name="inner_parts",
    )
    near, mid, far = (lax.ppermute(kv, both, route(d)) for d in (1, 2, 3))
    parts = lax.all_to_all(parts, "head", 0, 0)
    attn_out, inner_parts, part_up, grad_own, grad_near, grad_mid, grad_far = call(
        functools.partial(main_kernel, 2),
        [
            ((rows, width), BF16),
            ((n_head, r, rows), F32),
            ((r, width), F32),
            ((2, rows, HD), F32),
            ((2, rows, HD), BF16),
            ((2, rows, HD), BF16),
            ((2, rows, HD), BF16),
        ],
        parts,
        adapter_up,
        query_base,
        grad_out,
        kv,
        near,
        mid,
        far,
        scratch=[
            pltpu.VMEM((rows, width), BF16),
            pltpu.VMEM((keys, HD), BF16),
            pltpu.VMEM((keys, HD), BF16),
            pltpu.VMEM((HD, keys), BF16),
            pltpu.VMEM((HD, keys), BF16),
            pltpu.VMEM((width, rows), F32),
            pltpu.VMEM((keys, HD), F32),
            pltpu.VMEM((keys, HD), F32),
        ],
        limit=MAIN_VMEM,
        name="attention",
    )
    sent = [
        lax.ppermute(term, both, route(d, back=True))
        for d, term in ((1, grad_near), (2, grad_mid), (3, grad_far))
    ]
    inner_parts = lax.all_to_all(inner_parts, "head", 0, 0)

    wide = 16
    close = [[g * wide + m for m in range(wide)] for g in range(n_ctx // wide)]
    apart = [[g * wide + m for g in range(n_ctx // wide)] for m in range(wide)]
    close, apart = (ctx_groups(n_ctx, n_head, groups) for groups in (close, apart))
    piece = 2 * width // wide
    grad_embeddings, pieces = call(
        last_kernel,
        [((rows, width), F32), ((wide, r, piece), F32)],
        inner_parts,
        embeddings,
        down_t,
        part_up,
        name="grad_embeddings",
    )
    pieces = lax.all_to_all(pieces, both, 0, 0, axis_index_groups=close)
    mine = jnp.sum(pieces, axis=0)
    mine = jnp.broadcast_to(mine[None], (n_ctx // wide, *mine.shape))
    mine = lax.all_to_all(mine, both, 0, 0, axis_index_groups=apart)
    mine = jnp.sum(mine, axis=0)
    mine = jnp.broadcast_to(mine[None], (wide, *mine.shape))
    whole = lax.all_to_all(mine, both, 0, 0, axis_index_groups=close)
    whole = whole.transpose(1, 0, 2).reshape(r, 2 * width)
    grad_adapter_down, grad_adapter_up = whole[:, :width].T, whole[:, width:]

    received = grad_own
    for term in sent:
        received = received + term.astype(F32)
    return (
        attn_out,
        grad_embeddings,
        grad_adapter_down,
        grad_adapter_up,
        received[0],
        received[1],
    )


def solution(mesh):
    in_specs = (
        P("ctx", "head"),
        P("head", None),
        P(None, "head"),
        P("ctx", "head"),
        P("ctx", "head"),
        P("ctx", "head"),
        P("ctx", "head"),
    )
    out_specs = (
        P("ctx", "head"),
        P("ctx", "head"),
        P("head", None),
        P(None, "head"),
        P("ctx", "head"),
        P("ctx", "head"),
    )
    return jax.shard_map(
        on_device, mesh=mesh, in_specs=in_specs, out_specs=out_specs, check_vma=False
    )
```

```python
import functools
import math

import jax
import jax.numpy as jnp
from jax import lax
from jax.experimental import pallas as pl
from jax.experimental.pallas import tpu as pltpu
from jax.sharding import PartitionSpec as P

HD = 128
TIE = 0
HPS = 4
RM = 2
RH = 5
FIRST_LOW = 12
FIRST_HIGH = 0
TURN = 8
WIDE_BACK = False
SENT = jnp.float32
FIRST_VMEM = 16 * 2**20
SPAN = 4
FAR = 1e30
F32 = jnp.float32
BF16 = jnp.bfloat16
NT = (((1,), (1,)), ((), ()))
TN = (((0,), (0,)), ((), ()))
MAIN_VMEM = 40 * 2**20
SMALL_VMEM = 16 * 2**20


def dot(a, b, dims=(((1,), (0,)), ((), ()))):
    return lax.dot_general(a, b, dims, preferred_element_type=F32)


def split3(x):
    hi = x.astype(BF16).astype(F32)
    rest = x - hi
    mid = rest.astype(BF16).astype(F32)
    low = rest - mid
    return jnp.concatenate([hi, mid, low, jnp.zeros_like(x)], axis=0).astype(BF16)


def thrice(x):
    x = x.astype(F32)
    return jnp.concatenate([x, x, x, jnp.zeros_like(x)], axis=0).astype(BF16)


def first_kernel(emb_hbm, down_hbm, parts_ref, emb_ref, down_ref, sems):
    copies = [
        pltpu.make_async_copy(down_hbm, down_ref, sems.at[0]),
        pltpu.make_async_copy(emb_hbm, emb_ref, sems.at[1]),
    ]
    for copy in copies:
        copy.start()
    for copy in copies:
        copy.wait()
    part = dot(down_ref[...], emb_ref[...], NT)
    for peer in range(parts_ref.shape[0]):
        parts_ref[peer] = part


def second_kernel(parts_ref, key_ref, value_ref, cot_ref, kv_ref, cot_t_ref):
    kv_ref[0] = key_ref[...]
    kv_ref[1] = value_ref[...]
    for head in range(cot_ref.shape[1] // HD):
        at = slice(head * HD, (head + 1) * HD)
        cot_t_ref[at, :] = cot_ref[:, at].astype(F32).T.astype(BF16)


def main_kernel(
    heads_per_step,
    parts_ref,
    up_ref,
    base_ref,
    cot_ref,
    cot_t_ref,
    own_ref,
    near_ref,
    mid_ref,
    far_ref,
    attn_ref,
    inner_parts_ref,
    part_up_ref,
    grad_own_ref,
    grad_near_ref,
    grad_mid_ref,
    grad_far_ref,
    query_ref,
    key_ref,
    value_ref,
    key_t_ref,
    value_t_ref,
    grad_q_ref,
    acc_k_ref,
    acc_v_ref,
):
    rows = base_ref.shape[0]
    heads = base_ref.shape[1] // HD
    inv_scale = 1.0 / math.sqrt(HD)
    to_exp2 = inv_scale * math.log2(math.e)
    n_head = lax.axis_size("head")
    shift = jnp.where(lax.axis_index("head") >= n_head // 2, SPAN // 2, 0)
    rank = lax.rem(lax.axis_index("ctx") + SPAN - shift, SPAN)

    inner = jnp.sum(parts_ref[...], axis=0)
    inner3 = split3(inner)
    for position, ref in enumerate((far_ref, mid_ref, near_ref, own_ref)):
        at = slice(position * rows, (position + 1) * rows)
        key_ref[at, :] = ref[0]
        value_ref[at, :] = ref[1]
        key_t_ref[:, at] = ref[0].astype(F32).T.astype(BF16)
        value_t_ref[:, at] = ref[1].astype(F32).T.astype(BF16)
    acc_k_ref[...] = jnp.zeros_like(acc_k_ref)
    acc_v_ref[...] = jnp.zeros_like(acc_v_ref)

    query_ref[...] = (
        base_ref[...].astype(F32) + 2.0 * dot(inner3, thrice(up_ref[...]), TN)
    ).astype(BF16)
    source = lax.broadcasted_iota(jnp.int32, (rows, rows), 0)
    target = lax.broadcasted_iota(jnp.int32, (rows, rows), 1)
    causal = source <= target
    closed = [jnp.where(rank >= SPAN - 1 - p, 0.0, FAR) for p in range(SPAN - 1)]

    spans = [slice(p * rows, (p + 1) * rows) for p in range(SPAN)]

    def one_head(head):
        at = pl.ds(pl.multiple_of(head * HD, HD), HD)
        query, cot = query_ref[:, at], cot_ref[:, at]
        blocks = [dot(key_ref[span, :], query, NT) for span in spans]
        blocks[-1] = jnp.where(causal, blocks[-1], -FAR)
        tops = [jnp.max(block, axis=0, keepdims=True) for block in blocks]
        top = tops[-1]
        for p in range(SPAN - 1):
            top = jnp.maximum(top, tops[p] - closed[p])
        limits = [top + closed[p] for p in range(SPAN - 1)] + [top]
        powers = [jnp.exp2((b - t) * to_exp2) for b, t in zip(blocks, limits)]
        total = sum(jnp.sum(power, axis=0, keepdims=True) for power in powers)
        inverse = 1.0 / total
        weights = [power * inverse for power in powers]
        weights_b = [weight.astype(BF16) for weight in weights]
        attn_t = sum(dot(value_t_ref[:, span], w) for span, w in zip(spans, weights_b))
        delta = jnp.sum(cot_t_ref[at, :].astype(F32) * attn_t, axis=0, keepdims=True)
        attn_ref[:, at] = attn_t.T.astype(BF16)
        dscores = []
        for span, weight in zip(spans, weights):
            dprob = dot(value_ref[span, :], cot, NT)
            dscores.append((weight * (dprob - delta)).astype(BF16))
        grad_q = sum(dot(key_t_ref[:, span], d) for span, d in zip(spans, dscores))
        grad_q_ref[at, :] = grad_q * (2.0 * inv_scale)
        return query, cot, weights_b, dscores

    def step(i, carry):
        got = [one_head(i * heads_per_step + j) for j in range(heads_per_step)]
        query, cot = (jnp.concatenate([g[k] for g in got], axis=0) for k in (0, 1))
        for p, span in enumerate(spans):
            weight_b, dscore = (
                jnp.concatenate([g[k][p] for g in got], axis=1) for k in (2, 3)
            )
            acc_v_ref[span, :] += dot(weight_b, cot)
            acc_k_ref[span, :] += dot(dscore, query)
        return carry

    lax.fori_loop(0, heads // heads_per_step, step, 0)

    outs = (grad_far_ref, grad_mid_ref, grad_near_ref, grad_own_ref)
    for position, ref in enumerate(outs):
        at = slice(position * rows, (position + 1) * rows)
        ref[0] = (acc_k_ref[at, :] * inv_scale).astype(ref.dtype)
        ref[1] = acc_v_ref[at, :].astype(ref.dtype)

    grad_q = grad_q_ref[...]
    high = grad_q.astype(BF16)
    low = (grad_q - high.astype(F32)).astype(BF16)
    up = up_ref[...]
    grad_inner = dot(up, high) + dot(up, low)
    for peer in range(inner_parts_ref.shape[0]):
        inner_parts_ref[peer] = grad_inner
    r = inner.shape[0]
    rows3 = dot(inner3, high, NT)
    part_up = rows3[:r] + rows3[r : 2 * r] + rows3[2 * r : 3 * r]
    rows3 = dot(inner3, low, NT)
    part_up_ref[...] = part_up + rows3[:r] + rows3[r : 2 * r]


def pieces_kernel(parts_ref, emb_ref, part_up_ref, pieces_ref, terms_ref):
    grad_inner = jnp.sum(parts_ref[...], axis=0)
    r = grad_inner.shape[0]
    terms = split3(grad_inner)
    terms_ref[...] = terms
    rows3 = dot(terms, emb_ref[...])
    part_down = rows3[:r] + rows3[r : 2 * r] + rows3[2 * r : 3 * r]
    half = pieces_ref.shape[0] // 2
    width = pieces_ref.shape[2]
    for piece in range(half):
        at = slice(piece * width, (piece + 1) * width)
        pieces_ref[(piece + TURN) % (2 * half)] = part_down[:, at]
        pieces_ref[(half + piece + TURN) % (2 * half)] = part_up_ref[:, at]


def grad_emb_kernel(terms_ref, down_ref, grad_emb_ref):
    grad_emb_ref[...] = dot(terms_ref[...], thrice(down_ref[...]), TN)


def call(kernel, outs, *args, own=(), scratch=(), limit=SMALL_VMEM, name=None):
    specs = [
        pl.BlockSpec(memory_space=pltpu.HBM if i in own else pltpu.VMEM)
        for i in range(len(args))
    ]
    return pl.pallas_call(
        kernel,
        out_shape=[jax.ShapeDtypeStruct(shape, dtype) for shape, dtype in outs],
        in_specs=specs,
        scratch_shapes=scratch,
        compiler_params=pltpu.CompilerParams(vmem_limit_bytes=limit),
        name=name,
    )(*args)


def ctx_groups(n_ctx, n_head, members):
    return [[c * n_head + h for c in group] for group in members for h in range(n_head)]


def attention(parts, adapter_up, query_base, grad_out, cot_t, kv, near, mid, far):
    rows, width = query_base.shape
    n_head, r, _ = parts.shape
    keys = SPAN * rows
    return call(
        functools.partial(main_kernel, HPS),
        [
            ((rows, width), BF16),
            ((n_head, r, rows), F32),
            ((r, width), F32),
            ((2, rows, HD), F32),
            ((2, rows, HD), BF16),
            ((2, rows, HD), BF16),
            ((2, rows, HD), BF16),
        ],
        parts,
        adapter_up,
        query_base,
        grad_out,
        cot_t,
        kv,
        near,
        mid,
        far,
        scratch=[
            pltpu.VMEM((rows, width), BF16),
            pltpu.VMEM((keys, HD), BF16),
            pltpu.VMEM((keys, HD), BF16),
            pltpu.VMEM((HD, keys), BF16),
            pltpu.VMEM((HD, keys), BF16),
            pltpu.VMEM((width, rows), F32),
            pltpu.VMEM((keys, HD), F32),
            pltpu.VMEM((keys, HD), F32),
        ],
        limit=MAIN_VMEM,
        name="attention",
    )


def heads_of(n_ctx, n_head):
    order = [(h + RH) % n_head for h in range(n_head)]
    return [[c * n_head + h for h in order] for c in range(n_ctx)]


def on_device(embeddings, adapter_down, adapter_up, query_base, key_states, values, grad_out):
    rows, width = query_base.shape
    r = adapter_up.shape[0]
    n_ctx, n_head = lax.axis_size("ctx"), lax.axis_size("head")
    both = ("ctx", "head")
    keys = SPAN * rows
    down_t = adapter_down.T

    def route(distance, back=False):
        pairs = []
        for head in range(n_head):
            shift = SPAN // 2 if head >= n_head // 2 else 0
            for ctx in range(n_ctx):
                if (ctx - shift) % SPAN + distance < SPAN:
                    pair = (ctx * n_head + head, (ctx + distance) % n_ctx * n_head + head)
                    pairs.append(pair[::-1] if back else pair)
        return pairs

    (parts,) = call(
        first_kernel,
        [((n_head, r, rows), F32)],
        embeddings,
        down_t,
        own=(0, 1),
        scratch=[
            pltpu.VMEM(embeddings.shape, BF16),
            pltpu.VMEM(down_t.shape, BF16),
            pltpu.SemaphoreType.DMA((2,)),
        ],
        limit=FIRST_VMEM,
        name="inner_parts",
    )
    kv, cot_t = call(
        second_kernel,
        [((2, rows, HD), BF16), ((width, rows), BF16)],
        parts,
        key_states,
        values,
        grad_out,
        own=(0,),
        name="pack",
    )
    near, mid, far = (lax.ppermute(kv, both, route(d)) for d in (1, 2, 3))
    parts = lax.all_to_all(parts, both, 0, 0, axis_index_groups=heads_of(n_ctx, n_head))
    attn_out, inner_parts, part_up, grad_own, grad_near, grad_mid, grad_far = attention(
        parts, adapter_up, query_base, grad_out, cot_t, kv, near, mid, far
    )
    inner_parts = lax.all_to_all(inner_parts, both, 0, 0, axis_index_groups=heads_of(n_ctx, n_head))

    wide = 16
    blocks = n_ctx // wide
    first_of = [FIRST_LOW if g < blocks // 2 else FIRST_HIGH for g in range(blocks)]
    lists = [
        [g * wide + (m + first_of[g]) % wide for m in range(wide)] for g in range(blocks)
    ]
    block_order = [(g + RM) % blocks for g in range(blocks)]
    every = [[c for g in block_order for c in lists[g]]]
    apart = [[lists[g][m] for g in block_order] for m in range(wide)]
    back = [
        [g * wide + (m + first_of[g] + TURN) % wide for m in range(wide)]
        for g in range(blocks)
    ]
    close, apart, every, back = (
        ctx_groups(n_ctx, n_head, groups) for groups in (lists, apart, every, back)
    )
    piece = 2 * width // wide
    pieces, terms = call(
        pieces_kernel,
        [((wide, r, piece), F32), ((4 * r, rows), BF16)],
        inner_parts,
        embeddings,
        part_up,
        name="adapter_parts",
    )
    (grad_embeddings,) = call(
        grad_emb_kernel,
        [((rows, width), F32)],
        terms,
        down_t,
        name="grad_embeddings",
    )

    def send_terms(after):
        terms = (grad_near, grad_mid, grad_far)
        if after is not None:
            after, *terms = lax.optimization_barrier((after, *terms))
        sent = [
            lax.ppermute(term, both, route(d, back=True))
            for d, term in zip((1, 2, 3), terms)
        ]
        return after, sent

    if TIE == 0:
        _, sent = send_terms(None)
    if TIE == 3:
        _, sent = send_terms(None)
        pieces, *sent = lax.optimization_barrier((pieces, *sent))
    pieces = lax.all_to_all(pieces, both, 0, 0, axis_index_groups=close)
    mine = jnp.sum(pieces, axis=0)
    if TIE == 1:
        mine, sent = send_terms(mine)
    if WIDE_BACK:
        mine = jnp.broadcast_to(mine[None].astype(SENT), (n_ctx, *mine.shape))
        whole = lax.all_to_all(mine, both, 0, 0, axis_index_groups=every)
        whole = jnp.sum(whole.reshape(blocks, wide, r, piece).astype(F32), axis=0)
    else:
        mine = jnp.broadcast_to(mine[None], (blocks, *mine.shape))
        mine = lax.all_to_all(mine, both, 0, 0, axis_index_groups=apart)
        mine = jnp.sum(mine, axis=0)
        mine = jnp.broadcast_to(mine[None], (wide, *mine.shape))
        whole = lax.all_to_all(mine, both, 0, 0, axis_index_groups=back)
    whole = whole.transpose(1, 0, 2).reshape(r, 2 * width)
    grad_adapter_down, grad_adapter_up = whole[:, :width].T, whole[:, width:]

    received = grad_own
    for term in sent:
        received = received + term.astype(F32)
    return (
        attn_out,
        grad_embeddings,
        grad_adapter_down,
        grad_adapter_up,
        received[0],
        received[1],
    )


def solution(mesh):
    in_specs = (
        P("ctx", "head"),
        P("head", None),
        P(None, "head"),
        P("ctx", "head"),
        P("ctx", "head"),
        P("ctx", "head"),
        P("ctx", "head"),
    )
    out_specs = (
        P("ctx", "head"),
        P("ctx", "head"),
        P("head", None),
        P(None, "head"),
        P("ctx", "head"),
        P("ctx", "head"),
    )
    return jax.shard_map(
        on_device, mesh=mesh, in_specs=in_specs, out_specs=out_specs, check_vma=False
    )
```

```python
import functools
import math

import jax
import jax.numpy as jnp
from jax import lax
from jax.experimental import pallas as pl
from jax.experimental.pallas import tpu as pltpu
from jax.sharding import PartitionSpec as P

HD = 128
TIE = 0
HPS = 4
RM = 2
RH = 5
FIRST_LOW = 12
FIRST_HIGH = 8
TURN = 0
WIDE_BACK = True
SENT = jnp.bfloat16
FIRST_VMEM = 60 * 2**20
TURN_COST = 0
Q_COST = 0
EMB_COST = 0
SPAN = 4
FAR = 1e30
F32 = jnp.float32
BF16 = jnp.bfloat16
NT = (((1,), (1,)), ((), ()))
TN = (((0,), (0,)), ((), ()))
MAIN_VMEM = 40 * 2**20
SMALL_VMEM = 16 * 2**20


def dot(a, b, dims=(((1,), (0,)), ((), ()))):
    return lax.dot_general(a, b, dims, preferred_element_type=F32)


def split3(x):
    hi = x.astype(BF16).astype(F32)
    rest = x - hi
    mid = rest.astype(BF16).astype(F32)
    low = rest - mid
    return jnp.concatenate([hi, mid, low, jnp.zeros_like(x)], axis=0).astype(BF16)


def thrice(x):
    x = x.astype(F32)
    return jnp.concatenate([x, x, x, jnp.zeros_like(x)], axis=0).astype(BF16)


def first_kernel(
    emb_hbm, down_hbm, key_hbm, value_hbm, parts_ref, kv_ref, emb_ref, down_ref, sems
):
    pairs = (
        (down_hbm, down_ref),
        (emb_hbm, emb_ref),
        (key_hbm, kv_ref.at[0]),
        (value_hbm, kv_ref.at[1]),
    )
    copies = [pltpu.make_async_copy(a, b, sems.at[i]) for i, (a, b) in enumerate(pairs)]
    for copy in copies:
        copy.start()
    copies[0].wait()
    copies[1].wait()
    part = dot(down_ref[...], emb_ref[...], NT)
    for peer in range(parts_ref.shape[0]):
        parts_ref[peer] = part
    copies[2].wait()
    copies[3].wait()


def final_kernel(whole_ref, own_ref, near_ref, mid_ref, far_ref, *outs):
    down_ref, up_ref, grad_key_ref, grad_value_ref = outs
    pieces, _, width = whole_ref.shape
    half = pieces // 2
    for piece in range(half):
        at = slice(piece * width, (piece + 1) * width)
        down_ref[:, at] = whole_ref[piece]
        up_ref[:, at] = whole_ref[half + piece]
    for i, ref in enumerate((grad_key_ref, grad_value_ref)):
        terms = [term[i].astype(F32) for term in (near_ref, mid_ref, far_ref)]
        ref[...] = own_ref[i] + terms[0] + terms[1] + terms[2]


def turn_kernel(
    own_ref, near_ref, mid_ref, far_ref, cot_ref, key_ref, value_ref, key_t_ref, value_t_ref, cot_t_ref
):
    rows = own_ref.shape[1]
    for position, ref in enumerate((far_ref, mid_ref, near_ref, own_ref)):
        at = slice(position * rows, (position + 1) * rows)
        key_ref[at, :] = ref[0]
        value_ref[at, :] = ref[1]
        key_t_ref[:, at] = ref[0].astype(F32).T.astype(BF16)
        value_t_ref[:, at] = ref[1].astype(F32).T.astype(BF16)
    for head in range(cot_ref.shape[1] // HD):
        at = slice(head * HD, (head + 1) * HD)
        cot_t_ref[at, :] = cot_ref[:, at].astype(F32).T.astype(BF16)


def spread_kernel(terms_ref, out_ref):
    total = jnp.sum(terms_ref[...], axis=0)
    for peer in range(out_ref.shape[0]):
        out_ref[peer] = total.astype(out_ref.dtype)


def main_kernel(
    heads_per_step,
    parts_ref,
    up_ref,
    base_ref,
    cot_ref,
    cot_t_ref,
    key_ref,
    value_ref,
    key_t_ref,
    value_t_ref,
    attn_ref,
    inner_parts_ref,
    part_up_ref,
    grad_own_ref,
    grad_near_ref,
    grad_mid_ref,
    grad_far_ref,
    query_ref,
    grad_q_ref,
    acc_k_ref,
    acc_v_ref,
):
    rows = base_ref.shape[0]
    heads = base_ref.shape[1] // HD
    inv_scale = 1.0 / math.sqrt(HD)
    to_exp2 = inv_scale * math.log2(math.e)
    n_head = lax.axis_size("head")
    shift = jnp.where(lax.axis_index("head") >= n_head // 2, SPAN // 2, 0)
    rank = lax.rem(lax.axis_index("ctx") + SPAN - shift, SPAN)

    inner3 = split3(jnp.sum(parts_ref[...], axis=0))
    query_ref[...] = (
        base_ref[...].astype(F32) + 2.0 * dot(inner3, thrice(up_ref[...]), TN)
    ).astype(BF16)
    acc_k_ref[...] = jnp.zeros_like(acc_k_ref)
    acc_v_ref[...] = jnp.zeros_like(acc_v_ref)

    source = lax.broadcasted_iota(jnp.int32, (rows, rows), 0)
    target = lax.broadcasted_iota(jnp.int32, (rows, rows), 1)
    causal = source <= target
    closed = [jnp.where(rank >= SPAN - 1 - p, 0.0, FAR) for p in range(SPAN - 1)]

    spans = [slice(p * rows, (p + 1) * rows) for p in range(SPAN)]

    def one_head(head):
        at = pl.ds(pl.multiple_of(head * HD, HD), HD)
        query, cot = query_ref[:, at], cot_ref[:, at]
        blocks = [dot(key_ref[span, :], query, NT) for span in spans]
        blocks[-1] = jnp.where(causal, blocks[-1], -FAR)
        tops = [jnp.max(block, axis=0, keepdims=True) for block in blocks]
        top = tops[-1]
        for p in range(SPAN - 1):
            top = jnp.maximum(top, tops[p] - closed[p])
        limits = [top + closed[p] for p in range(SPAN - 1)] + [top]
        powers = [jnp.exp2((b - t) * to_exp2) for b, t in zip(blocks, limits)]
        total = sum(jnp.sum(power, axis=0, keepdims=True) for power in powers)
        inverse = 1.0 / total
        weights = [power * inverse for power in powers]
        weights_b = [weight.astype(BF16) for weight in weights]
        attn_t = sum(dot(value_t_ref[:, span], w) for span, w in zip(spans, weights_b))
        delta = jnp.sum(cot_t_ref[at, :].astype(F32) * attn_t, axis=0, keepdims=True)
        attn_ref[:, at] = attn_t.T.astype(BF16)
        dscores = []
        for span, weight in zip(spans, weights):
            dprob = dot(value_ref[span, :], cot, NT)
            dscores.append((weight * (dprob - delta)).astype(BF16))
        grad_q = sum(dot(key_t_ref[:, span], d) for span, d in zip(spans, dscores))
        grad_q_ref[at, :] = grad_q * (2.0 * inv_scale)
        return query, cot, weights_b, dscores

    def step(i, carry):
        got = [one_head(i * heads_per_step + j) for j in range(heads_per_step)]
        query, cot = (jnp.concatenate([g[k] for g in got], axis=0) for k in (0, 1))
        for p, span in enumerate(spans):
            weight_b, dscore = (
                jnp.concatenate([g[k][p] for g in got], axis=1) for k in (2, 3)
            )
            acc_v_ref[span, :] += dot(weight_b, cot)
            acc_k_ref[span, :] += dot(dscore, query)
        return carry

    lax.fori_loop(0, heads // heads_per_step, step, 0)

    outs = (grad_far_ref, grad_mid_ref, grad_near_ref, grad_own_ref)
    for position, ref in enumerate(outs):
        at = slice(position * rows, (position + 1) * rows)
        ref[0] = (acc_k_ref[at, :] * inv_scale).astype(ref.dtype)
        ref[1] = acc_v_ref[at, :].astype(ref.dtype)

    grad_q = grad_q_ref[...]
    high = grad_q.astype(BF16)
    low = (grad_q - high.astype(F32)).astype(BF16)
    up = up_ref[...]
    grad_inner = dot(up, high) + dot(up, low)
    for peer in range(inner_parts_ref.shape[0]):
        inner_parts_ref[peer] = grad_inner
    r = up.shape[0]
    rows3 = dot(inner3, high, NT)
    part_up = rows3[:r] + rows3[r : 2 * r] + rows3[2 * r : 3 * r]
    rows3 = dot(inner3, low, NT)
    part_up_ref[...] = part_up + rows3[:r] + rows3[r : 2 * r]


def pieces_kernel(parts_ref, emb_ref, part_up_ref, pieces_ref, terms_ref):
    grad_inner = jnp.sum(parts_ref[...], axis=0)
    r = grad_inner.shape[0]
    terms = split3(grad_inner)
    terms_ref[...] = terms
    rows3 = dot(terms, emb_ref[...])
    part_down = rows3[:r] + rows3[r : 2 * r] + rows3[2 * r : 3 * r]
    half = pieces_ref.shape[0] // 2
    width = pieces_ref.shape[2]
    for piece in range(half):
        at = slice(piece * width, (piece + 1) * width)
        pieces_ref[(piece + TURN) % (2 * half)] = part_down[:, at]
        pieces_ref[(half + piece + TURN) % (2 * half)] = part_up_ref[:, at]


def grad_emb_kernel(terms_ref, down_ref, grad_emb_ref):
    grad_emb_ref[...] = dot(terms_ref[...], thrice(down_ref[...]), TN)


def call(
    kernel, outs, *args, own=(), own_out=(), scratch=(), limit=SMALL_VMEM, cost=0, name=None
):
    specs = [
        pl.BlockSpec(memory_space=pltpu.HBM if i in own else pltpu.VMEM)
        for i in range(len(args))
    ]
    return pl.pallas_call(
        kernel,
        out_shape=[jax.ShapeDtypeStruct(shape, dtype) for shape, dtype in outs],
        in_specs=specs,
        out_specs=[
            pl.BlockSpec(memory_space=pltpu.HBM if i in own_out else pltpu.VMEM)
            for i in range(len(outs))
        ],
        cost_estimate=pl.CostEstimate(flops=0, bytes_accessed=cost, transcendentals=0)
        if cost
        else None,
        scratch_shapes=scratch,
        compiler_params=pltpu.CompilerParams(vmem_limit_bytes=limit),
        name=name,
    )(*args)


def ctx_groups(n_ctx, n_head, members):
    return [[c * n_head + h for c in group] for group in members for h in range(n_head)]


def attention(parts, adapter_up, query_base, grad_out, turned):
    rows, width = query_base.shape
    n_head, r, _ = parts.shape
    keys = SPAN * rows
    return call(
        functools.partial(main_kernel, HPS),
        [
            ((rows, width), BF16),
            ((n_head, r, rows), F32),
            ((r, width), F32),
            ((2, rows, HD), F32),
            ((2, rows, HD), BF16),
            ((2, rows, HD), BF16),
            ((2, rows, HD), BF16),
        ],
        parts,
        adapter_up,
        query_base,
        grad_out,
        *turned,
        scratch=[
            pltpu.VMEM((rows, width), BF16),
            pltpu.VMEM((width, rows), F32),
            pltpu.VMEM((keys, HD), F32),
            pltpu.VMEM((keys, HD), F32),
        ],
        limit=MAIN_VMEM,
        name="attention",
    )


def spread(terms, peers, dtype):
    (out,) = call(
        spread_kernel, [((peers, *terms.shape[1:]), dtype)], terms, name="spread"
    )
    return out


def heads_of(n_ctx, n_head):
    order = [(h + RH) % n_head for h in range(n_head)]
    return [[c * n_head + h for h in order] for c in range(n_ctx)]


def on_device(embeddings, adapter_down, adapter_up, query_base, key_states, values, grad_out):
    rows, width = query_base.shape
    r = adapter_up.shape[0]
    n_ctx, n_head = lax.axis_size("ctx"), lax.axis_size("head")
    both = ("ctx", "head")
    keys = SPAN * rows
    down_t = adapter_down.T

    def route(distance, back=False):
        pairs = []
        for head in range(n_head):
            shift = SPAN // 2 if head >= n_head // 2 else 0
            for ctx in range(n_ctx):
                if (ctx - shift) % SPAN + distance < SPAN:
                    pair = (ctx * n_head + head, (ctx + distance) % n_ctx * n_head + head)
                    pairs.append(pair[::-1] if back else pair)
        return pairs

    parts, kv = call(
        first_kernel,
        [((n_head, r, rows), F32), ((2, rows, HD), BF16)],
        embeddings,
        down_t,
        key_states,
        values,
        own=(0, 1, 2, 3),
        scratch=[
            pltpu.VMEM(embeddings.shape, BF16),
            pltpu.VMEM(down_t.shape, BF16),
            pltpu.SemaphoreType.DMA((4,)),
        ],
        limit=FIRST_VMEM,
        name="inner_parts",
    )
    near, mid, far = (lax.ppermute(kv, both, route(d)) for d in (1, 2, 3))
    parts = lax.all_to_all(parts, both, 0, 0, axis_index_groups=heads_of(n_ctx, n_head))
    key, value, key_t, value_t, cot_t = call(
        turn_kernel,
        [
            ((keys, HD), BF16),
            ((keys, HD), BF16),
            ((HD, keys), BF16),
            ((HD, keys), BF16),
            ((width, rows), BF16),
        ],
        kv,
        near,
        mid,
        far,
        grad_out,
        name="turn",
    )
    attn_out, inner_parts, part_up, grad_own, grad_near, grad_mid, grad_far = attention(
        parts, adapter_up, query_base, grad_out, (cot_t, key, value, key_t, value_t)
    )
    inner_parts = lax.all_to_all(inner_parts, both, 0, 0, axis_index_groups=heads_of(n_ctx, n_head))

    wide = 16
    blocks = n_ctx // wide
    first_of = [FIRST_LOW if g < blocks // 2 else FIRST_HIGH for g in range(blocks)]
    lists = [
        [g * wide + (m + first_of[g]) % wide for m in range(wide)] for g in range(blocks)
    ]
    block_order = [(g + RM) % blocks for g in range(blocks)]
    every = [[c for g in block_order for c in lists[g]]]
    apart = [[lists[g][m] for g in block_order] for m in range(wide)]
    back = [
        [g * wide + (m + first_of[g] + TURN) % wide for m in range(wide)]
        for g in range(blocks)
    ]
    close, apart, every, back = (
        ctx_groups(n_ctx, n_head, groups) for groups in (lists, apart, every, back)
    )
    piece = 2 * width // wide
    pieces, terms = call(
        pieces_kernel,
        [((wide, r, piece), F32), ((4 * r, rows), BF16)],
        inner_parts,
        embeddings,
        part_up,
        name="adapter_parts",
    )
    (grad_embeddings,) = call(
        grad_emb_kernel,
        [((rows, width), F32)],
        terms,
        down_t,
        cost=EMB_COST,
        name="grad_embeddings",
    )

    def send_terms(after):
        terms = (grad_near, grad_mid, grad_far)
        if after is not None:
            after, *terms = lax.optimization_barrier((after, *terms))
        sent = [
            lax.ppermute(term, both, route(d, back=True))
            for d, term in zip((1, 2, 3), terms)
        ]
        return after, sent

    if TIE == 0:
        _, sent = send_terms(None)
    if TIE == 3:
        _, sent = send_terms(None)
        pieces, *sent = lax.optimization_barrier((pieces, *sent))
    pieces = lax.all_to_all(pieces, both, 0, 0, axis_index_groups=close)
    mine = pieces
    if TIE == 1:
        mine, sent = send_terms(mine)
    if WIDE_BACK:
        mine = spread(mine, n_ctx, SENT)
        whole = lax.all_to_all(mine, both, 0, 0, axis_index_groups=every)
        whole = jnp.sum(whole.reshape(blocks, wide, r, piece).astype(F32), axis=0)
    else:
        mine = spread(mine, blocks, F32)
        mine = lax.all_to_all(mine, both, 0, 0, axis_index_groups=apart)
        mine = spread(mine, wide, F32)
        whole = lax.all_to_all(mine, both, 0, 0, axis_index_groups=back)
    grad_down, grad_up, grad_key, grad_value = call(
        final_kernel,
        [((r, width), F32), ((r, width), F32), ((rows, HD), F32), ((rows, HD), F32)],
        whole,
        grad_own,
        *sent,
        name="final",
    )
    return (attn_out, grad_embeddings, grad_down.T, grad_up, grad_key, grad_value)


def solution(mesh):
    in_specs = (
        P("ctx", "head"),
        P("head", None),
        P(None, "head"),
        P("ctx", "head"),
        P("ctx", "head"),
        P("ctx", "head"),
        P("ctx", "head"),
    )
    out_specs = (
        P("ctx", "head"),
        P("ctx", "head"),
        P("head", None),
        P(None, "head"),
        P("ctx", "head"),
        P("ctx", "head"),
    )
    return jax.shard_map(
        on_device, mesh=mesh, in_specs=in_specs, out_specs=out_specs, check_vma=False
    )
```

```python
import functools
import math

import jax
import jax.numpy as jnp
from jax import lax
from jax.experimental import pallas as pl
from jax.experimental.pallas import tpu as pltpu
from jax.sharding import PartitionSpec as P

HD = 128
HEADS_PER_STEP = 8
FIRST_HEAD = 5
FIRST_BLOCK = 2
FIRST_LOW, FIRST_HIGH = 12, 0
TURN = 8
FIRST_VMEM = 60 * 2**20
SPAN = 4
FAR = 1e30
F32 = jnp.float32
BF16 = jnp.bfloat16
NT = (((1,), (1,)), ((), ()))
TN = (((0,), (0,)), ((), ()))
MAIN_VMEM = 40 * 2**20
SMALL_VMEM = 16 * 2**20


def dot(a, b, dims=(((1,), (0,)), ((), ()))):
    return lax.dot_general(a, b, dims, preferred_element_type=F32)


def split3(x):
    hi = x.astype(BF16).astype(F32)
    rest = x - hi
    mid = rest.astype(BF16).astype(F32)
    low = rest - mid
    return jnp.concatenate([hi, mid, low, jnp.zeros_like(x)], axis=0).astype(BF16)


def thrice(x):
    x = x.astype(F32)
    return jnp.concatenate([x, x, x, jnp.zeros_like(x)], axis=0).astype(BF16)


def first_kernel(
    emb_hbm, down_hbm, key_hbm, value_hbm, parts_ref, kv_ref, emb_ref, down_ref, sems
):
    pairs = (
        (down_hbm, down_ref),
        (emb_hbm, emb_ref),
        (key_hbm, kv_ref.at[0]),
        (value_hbm, kv_ref.at[1]),
    )
    copies = [pltpu.make_async_copy(a, b, sems.at[i]) for i, (a, b) in enumerate(pairs)]
    for copy in copies:
        copy.start()
    copies[0].wait()
    copies[1].wait()
    part = dot(down_ref[...], emb_ref[...], NT)
    for peer in range(parts_ref.shape[0]):
        parts_ref[peer] = part
    copies[2].wait()
    copies[3].wait()


def turn_kernel(cot_ref, cot_t_ref):
    for head in range(cot_ref.shape[1] // HD):
        at = slice(head * HD, (head + 1) * HD)
        cot_t_ref[at, :] = cot_ref[:, at].astype(F32).T.astype(BF16)


def spread_kernel(terms_ref, out_ref):
    total = jnp.sum(terms_ref[...], axis=0)
    for peer in range(out_ref.shape[0]):
        out_ref[peer] = total


def main_kernel(
    heads_per_step,
    parts_ref,
    up_ref,
    base_ref,
    cot_ref,
    cot_t_ref,
    own_ref,
    near_ref,
    mid_ref,
    far_ref,
    attn_ref,
    inner_parts_ref,
    part_up_ref,
    grad_own_ref,
    grad_near_ref,
    grad_mid_ref,
    grad_far_ref,
    query_ref,
    key_ref,
    value_ref,
    key_t_ref,
    value_t_ref,
    grad_q_ref,
    acc_k_ref,
    acc_v_ref,
):
    rows = base_ref.shape[0]
    heads = base_ref.shape[1] // HD
    inv_scale = 1.0 / math.sqrt(HD)
    to_exp2 = inv_scale * math.log2(math.e)
    n_head = lax.axis_size("head")
    shift = jnp.where(lax.axis_index("head") >= n_head // 2, SPAN // 2, 0)
    rank = lax.rem(lax.axis_index("ctx") + SPAN - shift, SPAN)

    inner = jnp.sum(parts_ref[...], axis=0)
    inner3 = split3(inner)
    for position, ref in enumerate((far_ref, mid_ref, near_ref, own_ref)):
        at = slice(position * rows, (position + 1) * rows)
        key_ref[at, :] = ref[0]
        value_ref[at, :] = ref[1]
        key_t_ref[:, at] = ref[0].astype(F32).T.astype(BF16)
        value_t_ref[:, at] = ref[1].astype(F32).T.astype(BF16)
    acc_k_ref[...] = jnp.zeros_like(acc_k_ref)
    acc_v_ref[...] = jnp.zeros_like(acc_v_ref)

    query_ref[...] = (
        base_ref[...].astype(F32) + 2.0 * dot(inner3, thrice(up_ref[...]), TN)
    ).astype(BF16)
    source = lax.broadcasted_iota(jnp.int32, (rows, rows), 0)
    target = lax.broadcasted_iota(jnp.int32, (rows, rows), 1)
    causal = source <= target
    closed = [jnp.where(rank >= SPAN - 1 - p, 0.0, FAR) for p in range(SPAN - 1)]

    spans = [slice(p * rows, (p + 1) * rows) for p in range(SPAN)]

    def one_head(head):
        at = pl.ds(pl.multiple_of(head * HD, HD), HD)
        query, cot = query_ref[:, at], cot_ref[:, at]
        blocks = [dot(key_ref[span, :], query, NT) for span in spans]
        blocks[-1] = jnp.where(causal, blocks[-1], -FAR)
        tops = [jnp.max(block, axis=0, keepdims=True) for block in blocks]
        top = tops[-1]
        for p in range(SPAN - 1):
            top = jnp.maximum(top, tops[p] - closed[p])
        limits = [top + closed[p] for p in range(SPAN - 1)] + [top]
        powers = [jnp.exp2((b - t) * to_exp2) for b, t in zip(blocks, limits)]
        total = sum(jnp.sum(power, axis=0, keepdims=True) for power in powers)
        inverse = 1.0 / total
        weights = [power * inverse for power in powers]
        weights_b = [weight.astype(BF16) for weight in weights]
        attn_t = sum(dot(value_t_ref[:, span], w) for span, w in zip(spans, weights_b))
        delta = jnp.sum(cot_t_ref[at, :].astype(F32) * attn_t, axis=0, keepdims=True)
        attn_ref[:, at] = attn_t.T.astype(BF16)
        dscores = []
        for span, weight in zip(spans, weights):
            dprob = dot(value_ref[span, :], cot, NT)
            dscores.append((weight * (dprob - delta)).astype(BF16))
        grad_q = sum(dot(key_t_ref[:, span], d) for span, d in zip(spans, dscores))
        grad_q_ref[at, :] = grad_q * (2.0 * inv_scale)
        return query, cot, weights_b, dscores

    def step(i, carry):
        got = [one_head(i * heads_per_step + j) for j in range(heads_per_step)]
        query, cot = (jnp.concatenate([g[k] for g in got], axis=0) for k in (0, 1))
        for p, span in enumerate(spans):
            weight_b, dscore = (
                jnp.concatenate([g[k][p] for g in got], axis=1) for k in (2, 3)
            )
            acc_v_ref[span, :] += dot(weight_b, cot)
            acc_k_ref[span, :] += dot(dscore, query)
        return carry

    lax.fori_loop(0, heads // heads_per_step, step, 0)

    outs = (grad_far_ref, grad_mid_ref, grad_near_ref, grad_own_ref)
    for position, ref in enumerate(outs):
        at = slice(position * rows, (position + 1) * rows)
        ref[0] = (acc_k_ref[at, :] * inv_scale).astype(ref.dtype)
        ref[1] = acc_v_ref[at, :].astype(ref.dtype)

    grad_q = grad_q_ref[...]
    high = grad_q.astype(BF16)
    low = (grad_q - high.astype(F32)).astype(BF16)
    up = up_ref[...]
    grad_inner = dot(up, high) + dot(up, low)
    for peer in range(inner_parts_ref.shape[0]):
        inner_parts_ref[peer] = grad_inner
    r = inner.shape[0]
    rows3 = dot(inner3, high, NT)
    part_up = rows3[:r] + rows3[r : 2 * r] + rows3[2 * r : 3 * r]
    rows3 = dot(inner3, low, NT)
    part_up_ref[...] = part_up + rows3[:r] + rows3[r : 2 * r]


def pieces_kernel(parts_ref, emb_ref, part_up_ref, pieces_ref, terms_ref):
    grad_inner = jnp.sum(parts_ref[...], axis=0)
    r = grad_inner.shape[0]
    terms = split3(grad_inner)
    terms_ref[...] = terms
    rows3 = dot(terms, emb_ref[...])
    part_down = rows3[:r] + rows3[r : 2 * r] + rows3[2 * r : 3 * r]
    half = pieces_ref.shape[0] // 2
    width = pieces_ref.shape[2]
    for piece in range(half):
        at = slice(piece * width, (piece + 1) * width)
        pieces_ref[(piece + TURN) % (2 * half)] = part_down[:, at]
        pieces_ref[(half + piece + TURN) % (2 * half)] = part_up_ref[:, at]


def grad_emb_kernel(terms_ref, down_ref, grad_emb_ref):
    grad_emb_ref[...] = dot(terms_ref[...], thrice(down_ref[...]), TN)


def call(kernel, outs, *args, own=(), scratch=(), limit=SMALL_VMEM, name=None):
    specs = [
        pl.BlockSpec(memory_space=pltpu.HBM if i in own else pltpu.VMEM)
        for i in range(len(args))
    ]
    return pl.pallas_call(
        kernel,
        out_shape=[jax.ShapeDtypeStruct(shape, dtype) for shape, dtype in outs],
        in_specs=specs,
        scratch_shapes=scratch,
        compiler_params=pltpu.CompilerParams(vmem_limit_bytes=limit),
        name=name,
    )(*args)


def ctx_groups(n_ctx, n_head, members):
    return [[c * n_head + h for c in group] for group in members for h in range(n_head)]


def attention(parts, adapter_up, query_base, grad_out, cot_t, kv, near, mid, far):
    rows, width = query_base.shape
    n_head, r, _ = parts.shape
    keys = SPAN * rows
    return call(
        functools.partial(main_kernel, HEADS_PER_STEP),
        [
            ((rows, width), BF16),
            ((n_head, r, rows), F32),
            ((r, width), F32),
            ((2, rows, HD), F32),
            ((2, rows, HD), BF16),
            ((2, rows, HD), BF16),
            ((2, rows, HD), BF16),
        ],
        parts,
        adapter_up,
        query_base,
        grad_out,
        cot_t,
        kv,
        near,
        mid,
        far,
        scratch=[
            pltpu.VMEM((rows, width), BF16),
            pltpu.VMEM((keys, HD), BF16),
            pltpu.VMEM((keys, HD), BF16),
            pltpu.VMEM((HD, keys), BF16),
            pltpu.VMEM((HD, keys), BF16),
            pltpu.VMEM((width, rows), F32),
            pltpu.VMEM((keys, HD), F32),
            pltpu.VMEM((keys, HD), F32),
        ],
        limit=MAIN_VMEM,
        name="attention",
    )


def spread(terms, peers):
    (out,) = call(
        spread_kernel, [((peers, *terms.shape[1:]), F32)], terms, name="spread"
    )
    return out


def heads_of(n_ctx, n_head):
    order = [(h + FIRST_HEAD) % n_head for h in range(n_head)]
    return [[c * n_head + h for h in order] for c in range(n_ctx)]


def on_device(embeddings, adapter_down, adapter_up, query_base, key_states, values, grad_out):
    rows, width = query_base.shape
    r = adapter_up.shape[0]
    n_ctx, n_head = lax.axis_size("ctx"), lax.axis_size("head")
    both = ("ctx", "head")
    keys = SPAN * rows
    down_t = adapter_down.T

    def route(distance, back=False):
        pairs = []
        for head in range(n_head):
            shift = SPAN // 2 if head >= n_head // 2 else 0
            for ctx in range(n_ctx):
                if (ctx - shift) % SPAN + distance < SPAN:
                    pair = (ctx * n_head + head, (ctx + distance) % n_ctx * n_head + head)
                    pairs.append(pair[::-1] if back else pair)
        return pairs

    parts, kv = call(
        first_kernel,
        [((n_head, r, rows), F32), ((2, rows, HD), BF16)],
        embeddings,
        down_t,
        key_states,
        values,
        own=(0, 1, 2, 3),
        scratch=[
            pltpu.VMEM(embeddings.shape, BF16),
            pltpu.VMEM(down_t.shape, BF16),
            pltpu.SemaphoreType.DMA((4,)),
        ],
        limit=FIRST_VMEM,
        name="inner_parts",
    )
    (cot_t,) = call(
        turn_kernel, [((width, rows), BF16)], grad_out, name="turn"
    )
    near, mid, far = (lax.ppermute(kv, both, route(d)) for d in (1, 2, 3))
    parts = lax.all_to_all(parts, both, 0, 0, axis_index_groups=heads_of(n_ctx, n_head))
    attn_out, inner_parts, part_up, grad_own, grad_near, grad_mid, grad_far = attention(
        parts, adapter_up, query_base, grad_out, cot_t, kv, near, mid, far
    )
    sent = [
        lax.ppermute(term, both, route(d, back=True))
        for d, term in ((1, grad_near), (2, grad_mid), (3, grad_far))
    ]
    inner_parts = lax.all_to_all(inner_parts, both, 0, 0, axis_index_groups=heads_of(n_ctx, n_head))

    wide = 16
    blocks = n_ctx // wide
    first_of = [FIRST_LOW if g < blocks // 2 else FIRST_HIGH for g in range(blocks)]
    lists = [
        [g * wide + (m + first_of[g]) % wide for m in range(wide)] for g in range(blocks)
    ]
    block_order = [(g + FIRST_BLOCK) % blocks for g in range(blocks)]
    apart = [[lists[g][m] for g in block_order] for m in range(wide)]
    back = [
        [g * wide + (m + first_of[g] + TURN) % wide for m in range(wide)]
        for g in range(blocks)
    ]
    close, apart, back = (
        ctx_groups(n_ctx, n_head, groups) for groups in (lists, apart, back)
    )
    piece = 2 * width // wide
    pieces, terms = call(
        pieces_kernel,
        [((wide, r, piece), F32), ((4 * r, rows), BF16)],
        inner_parts,
        embeddings,
        part_up,
        name="adapter_parts",
    )
    (grad_embeddings,) = call(
        grad_emb_kernel,
        [((rows, width), F32)],
        terms,
        down_t,
        name="grad_embeddings",
    )

    pieces = lax.all_to_all(pieces, both, 0, 0, axis_index_groups=close)
    mine = spread(pieces, blocks)
    mine = lax.all_to_all(mine, both, 0, 0, axis_index_groups=apart)
    mine = spread(mine, wide)
    whole = lax.all_to_all(mine, both, 0, 0, axis_index_groups=back)
    whole = whole.transpose(1, 0, 2).reshape(r, 2 * width)
    grad_adapter_down, grad_adapter_up = whole[:, :width].T, whole[:, width:]

    received = grad_own
    for term in sent:
        received = received + term.astype(F32)
    return (
        attn_out,
        grad_embeddings,
        grad_adapter_down,
        grad_adapter_up,
        received[0],
        received[1],
    )


def solution(mesh):
    in_specs = (
        P("ctx", "head"),
        P("head", None),
        P(None, "head"),
        P("ctx", "head"),
        P("ctx", "head"),
        P("ctx", "head"),
        P("ctx", "head"),
    )
    out_specs = (
        P("ctx", "head"),
        P("ctx", "head"),
        P("head", None),
        P(None, "head"),
        P("ctx", "head"),
        P("ctx", "head"),
    )
    return jax.shard_map(
        on_device, mesh=mesh, in_specs=in_specs, out_specs=out_specs, check_vma=False
    )
```

```python
import functools
import math

import jax
import jax.numpy as jnp
from jax import lax
from jax.experimental import pallas as pl
from jax.experimental.pallas import tpu as pltpu
from jax.sharding import PartitionSpec as P

HD = 128
HEADS_PER_STEP = 8
FIRST_HEAD = 5
FIRST_BLOCK = 2
FIRST_LOW, FIRST_HIGH = 12, 12
TURN = 8
FIRST_VMEM = 60 * 2**20
SPAN = 4
FAR = 1e30
F32 = jnp.float32
BF16 = jnp.bfloat16
NT = (((1,), (1,)), ((), ()))
TN = (((0,), (0,)), ((), ()))
MAIN_VMEM = 40 * 2**20
SMALL_VMEM = 16 * 2**20


def dot(a, b, dims=(((1,), (0,)), ((), ()))):
    return lax.dot_general(a, b, dims, preferred_element_type=F32)


def split3(x):
    hi = x.astype(BF16).astype(F32)
    rest = x - hi
    mid = rest.astype(BF16).astype(F32)
    low = rest - mid
    return jnp.concatenate([hi, mid, low, jnp.zeros_like(x)], axis=0).astype(BF16)


def thrice(x):
    x = x.astype(F32)
    return jnp.concatenate([x, x, x, jnp.zeros_like(x)], axis=0).astype(BF16)


def first_kernel(
    emb_hbm, down_hbm, key_hbm, value_hbm, parts_ref, kv_ref, emb_ref, down_ref, sems
):
    pairs = (
        (down_hbm, down_ref),
        (emb_hbm, emb_ref),
        (key_hbm, kv_ref.at[0]),
        (value_hbm, kv_ref.at[1]),
    )
    copies = [pltpu.make_async_copy(a, b, sems.at[i]) for i, (a, b) in enumerate(pairs)]
    for copy in copies:
        copy.start()
    copies[0].wait()
    copies[1].wait()
    part = dot(down_ref[...], emb_ref[...], NT)
    for peer in range(parts_ref.shape[0]):
        parts_ref[peer] = part
    copies[2].wait()
    copies[3].wait()


def turn_kernel(cot_ref, cot_t_ref):
    for head in range(cot_ref.shape[1] // HD):
        at = slice(head * HD, (head + 1) * HD)
        cot_t_ref[at, :] = cot_ref[:, at].astype(F32).T.astype(BF16)


def spread_kernel(terms_ref, out_ref):
    total = jnp.sum(terms_ref[...], axis=0)
    for peer in range(out_ref.shape[0]):
        out_ref[peer] = total


def main_kernel(
    heads_per_step,
    parts_ref,
    up_ref,
    base_ref,
    cot_ref,
    cot_t_ref,
    own_ref,
    near_ref,
    mid_ref,
    far_ref,
    attn_ref,
    inner_parts_ref,
    part_up_ref,
    grad_own_ref,
    grad_near_ref,
    grad_mid_ref,
    grad_far_ref,
    query_ref,
    key_ref,
    value_ref,
    key_t_ref,
    value_t_ref,
    grad_q_ref,
    acc_k_ref,
    acc_v_ref,
):
    rows = base_ref.shape[0]
    heads = base_ref.shape[1] // HD
    inv_scale = 1.0 / math.sqrt(HD)
    to_exp2 = inv_scale * math.log2(math.e)
    n_head = lax.axis_size("head")
    shift = jnp.where(lax.axis_index("head") >= n_head // 2, SPAN // 2, 0)
    rank = lax.rem(lax.axis_index("ctx") + SPAN - shift, SPAN)

    inner = jnp.sum(parts_ref[...], axis=0)
    inner3 = split3(inner)
    for position, ref in enumerate((far_ref, mid_ref, near_ref, own_ref)):
        at = slice(position * rows, (position + 1) * rows)
        key_ref[at, :] = ref[0]
        value_ref[at, :] = ref[1]
        key_t_ref[:, at] = ref[0].astype(F32).T.astype(BF16)
        value_t_ref[:, at] = ref[1].astype(F32).T.astype(BF16)
    acc_k_ref[...] = jnp.zeros_like(acc_k_ref)
    acc_v_ref[...] = jnp.zeros_like(acc_v_ref)

    query_ref[...] = (
        base_ref[...].astype(F32) + 2.0 * dot(inner3, thrice(up_ref[...]), TN)
    ).astype(BF16)
    source = lax.broadcasted_iota(jnp.int32, (rows, rows), 0)
    target = lax.broadcasted_iota(jnp.int32, (rows, rows), 1)
    causal = source <= target
    closed = [jnp.where(rank >= SPAN - 1 - p, 0.0, FAR) for p in range(SPAN - 1)]

    spans = [slice(p * rows, (p + 1) * rows) for p in range(SPAN)]

    def one_head(head):
        at = pl.ds(pl.multiple_of(head * HD, HD), HD)
        query, cot = query_ref[:, at], cot_ref[:, at]
        blocks = [dot(key_ref[span, :], query, NT) for span in spans]
        blocks[-1] = jnp.where(causal, blocks[-1], -FAR)
        tops = [jnp.max(block, axis=0, keepdims=True) for block in blocks]
        top = tops[-1]
        for p in range(SPAN - 1):
            top = jnp.maximum(top, tops[p] - closed[p])
        limits = [top + closed[p] for p in range(SPAN - 1)] + [top]
        powers = [jnp.exp2((b - t) * to_exp2) for b, t in zip(blocks, limits)]
        total = sum(jnp.sum(power, axis=0, keepdims=True) for power in powers)
        inverse = 1.0 / total
        weights = [power * inverse for power in powers]
        weights_b = [weight.astype(BF16) for weight in weights]
        attn_t = sum(dot(value_t_ref[:, span], w) for span, w in zip(spans, weights_b))
        delta = jnp.sum(cot_t_ref[at, :].astype(F32) * attn_t, axis=0, keepdims=True)
        attn_ref[:, at] = attn_t.T.astype(BF16)
        dscores = []
        for span, weight in zip(spans, weights):
            dprob = dot(value_ref[span, :], cot, NT)
            dscores.append((weight * (dprob - delta)).astype(BF16))
        grad_q = sum(dot(key_t_ref[:, span], d) for span, d in zip(spans, dscores))
        grad_q_ref[at, :] = grad_q * (2.0 * inv_scale)
        return query, cot, weights_b, dscores

    def step(i, carry):
        got = [one_head(i * heads_per_step + j) for j in range(heads_per_step)]
        query, cot = (jnp.concatenate([g[k] for g in got], axis=0) for k in (0, 1))
        for p, span in enumerate(spans):
            weight_b, dscore = (
                jnp.concatenate([g[k][p] for g in got], axis=1) for k in (2, 3)
            )
            acc_v_ref[span, :] += dot(weight_b, cot)
            acc_k_ref[span, :] += dot(dscore, query)
        return carry

    lax.fori_loop(0, heads // heads_per_step, step, 0)

    outs = (grad_far_ref, grad_mid_ref, grad_near_ref, grad_own_ref)
    for position, ref in enumerate(outs):
        at = slice(position * rows, (position + 1) * rows)
        ref[0] = (acc_k_ref[at, :] * inv_scale).astype(ref.dtype)
        ref[1] = acc_v_ref[at, :].astype(ref.dtype)

    grad_q = grad_q_ref[...]
    high = grad_q.astype(BF16)
    low = (grad_q - high.astype(F32)).astype(BF16)
    up = up_ref[...]
    grad_inner = dot(up, high) + dot(up, low)
    for peer in range(inner_parts_ref.shape[0]):
        inner_parts_ref[peer] = grad_inner
    r = inner.shape[0]
    rows3 = dot(inner3, high, NT)
    part_up = rows3[:r] + rows3[r : 2 * r] + rows3[2 * r : 3 * r]
    rows3 = dot(inner3, low, NT)
    part_up_ref[...] = part_up + rows3[:r] + rows3[r : 2 * r]


def pieces_kernel(parts_ref, emb_ref, part_up_ref, pieces_ref, terms_ref):
    grad_inner = jnp.sum(parts_ref[...], axis=0)
    r = grad_inner.shape[0]
    terms = split3(grad_inner)
    terms_ref[...] = terms
    rows3 = dot(terms, emb_ref[...])
    part_down = rows3[:r] + rows3[r : 2 * r] + rows3[2 * r : 3 * r]
    half = pieces_ref.shape[0] // 2
    width = pieces_ref.shape[2]
    for piece in range(half):
        at = slice(piece * width, (piece + 1) * width)
        pieces_ref[(piece + TURN) % (2 * half)] = part_down[:, at]
        pieces_ref[(half + piece + TURN) % (2 * half)] = part_up_ref[:, at]


def grad_emb_kernel(terms_ref, down_ref, grad_emb_ref):
    grad_emb_ref[...] = dot(terms_ref[...], thrice(down_ref[...]), TN)


def call(kernel, outs, *args, own=(), scratch=(), limit=SMALL_VMEM, name=None):
    specs = [
        pl.BlockSpec(memory_space=pltpu.HBM if i in own else pltpu.VMEM)
        for i in range(len(args))
    ]
    return pl.pallas_call(
        kernel,
        out_shape=[jax.ShapeDtypeStruct(shape, dtype) for shape, dtype in outs],
        in_specs=specs,
        scratch_shapes=scratch,
        compiler_params=pltpu.CompilerParams(vmem_limit_bytes=limit),
        name=name,
    )(*args)


def ctx_groups(n_ctx, n_head, members):
    return [[c * n_head + h for c in group] for group in members for h in range(n_head)]


def attention(parts, adapter_up, query_base, grad_out, cot_t, kv, near, mid, far):
    rows, width = query_base.shape
    n_head, r, _ = parts.shape
    keys = SPAN * rows
    return call(
        functools.partial(main_kernel, HEADS_PER_STEP),
        [
            ((rows, width), BF16),
            ((n_head, r, rows), F32),
            ((r, width), F32),
            ((2, rows, HD), F32),
            ((2, rows, HD), BF16),
            ((2, rows, HD), BF16),
            ((2, rows, HD), BF16),
        ],
        parts,
        adapter_up,
        query_base,
        grad_out,
        cot_t,
        kv,
        near,
        mid,
        far,
        scratch=[
            pltpu.VMEM((rows, width), BF16),
            pltpu.VMEM((keys, HD), BF16),
            pltpu.VMEM((keys, HD), BF16),
            pltpu.VMEM((HD, keys), BF16),
            pltpu.VMEM((HD, keys), BF16),
            pltpu.VMEM((width, rows), F32),
            pltpu.VMEM((keys, HD), F32),
            pltpu.VMEM((keys, HD), F32),
        ],
        limit=MAIN_VMEM,
        name="attention",
    )


def spread(terms, peers):
    (out,) = call(
        spread_kernel, [((peers, *terms.shape[1:]), F32)], terms, name="spread"
    )
    return out


def heads_of(n_ctx, n_head):
    order = [(h + FIRST_HEAD) % n_head for h in range(n_head)]
    return [[c * n_head + h for h in order] for c in range(n_ctx)]


def on_device(embeddings, adapter_down, adapter_up, query_base, key_states, values, grad_out):
    rows, width = query_base.shape
    r = adapter_up.shape[0]
    n_ctx, n_head = lax.axis_size("ctx"), lax.axis_size("head")
    both = ("ctx", "head")
    keys = SPAN * rows
    down_t = adapter_down.T

    def route(distance, back=False):
        pairs = []
        for head in range(n_head):
            shift = SPAN // 2 if head >= n_head // 2 else 0
            for ctx in range(n_ctx):
                if (ctx - shift) % SPAN + distance < SPAN:
                    pair = (ctx * n_head + head, (ctx + distance) % n_ctx * n_head + head)
                    pairs.append(pair[::-1] if back else pair)
        return pairs

    parts, kv = call(
        first_kernel,
        [((n_head, r, rows), F32), ((2, rows, HD), BF16)],
        embeddings,
        down_t,
        key_states,
        values,
        own=(0, 1, 2, 3),
        scratch=[
            pltpu.VMEM(embeddings.shape, BF16),
            pltpu.VMEM(down_t.shape, BF16),
            pltpu.SemaphoreType.DMA((4,)),
        ],
        limit=FIRST_VMEM,
        name="inner_parts",
    )
    (cot_t,) = call(
        turn_kernel, [((width, rows), BF16)], grad_out, name="turn"
    )
    near, mid, far = (lax.ppermute(kv, both, route(d)) for d in (1, 2, 3))
    parts = lax.all_to_all(parts, both, 0, 0, axis_index_groups=heads_of(n_ctx, n_head))
    attn_out, inner_parts, part_up, grad_own, grad_near, grad_mid, grad_far = attention(
        parts, adapter_up, query_base, grad_out, cot_t, kv, near, mid, far
    )
    sent = [
        lax.ppermute(term, both, route(d, back=True))
        for d, term in ((1, grad_near), (2, grad_mid), (3, grad_far))
    ]
    inner_parts = lax.all_to_all(inner_parts, both, 0, 0, axis_index_groups=heads_of(n_ctx, n_head))

    wide = 16
    blocks = n_ctx // wide
    first_of = [FIRST_LOW if g < blocks // 2 else FIRST_HIGH for g in range(blocks)]
    lists = [
        [g * wide + (m + first_of[g]) % wide for m in range(wide)] for g in range(blocks)
    ]
    block_order = [(g + FIRST_BLOCK) % blocks for g in range(blocks)]
    apart = [[lists[g][m] for g in block_order] for m in range(wide)]
    back = [
        [g * wide + (m + first_of[g] + TURN) % wide for m in range(wide)]
        for g in range(blocks)
    ]
    close, apart, back = (
        ctx_groups(n_ctx, n_head, groups) for groups in (lists, apart, back)
    )
    piece = 2 * width // wide
    pieces, terms = call(
        pieces_kernel,
        [((wide, r, piece), F32), ((4 * r, rows), BF16)],
        inner_parts,
        embeddings,
        part_up,
        name="adapter_parts",
    )
    (grad_embeddings,) = call(
        grad_emb_kernel,
        [((rows, width), F32)],
        terms,
        down_t,
        name="grad_embeddings",
    )

    pieces = lax.all_to_all(pieces, both, 0, 0, axis_index_groups=close)
    mine = spread(pieces, blocks)
    mine = lax.all_to_all(mine, both, 0, 0, axis_index_groups=apart)
    mine = spread(mine, wide)
    whole = lax.all_to_all(mine, both, 0, 0, axis_index_groups=back)
    whole = whole.transpose(1, 0, 2).reshape(r, 2 * width)
    grad_adapter_down, grad_adapter_up = whole[:, :width].T, whole[:, width:]

    received = grad_own
    for term in sent:
        received = received + term.astype(F32)
    return (
        attn_out,
        grad_embeddings,
        grad_adapter_down,
        grad_adapter_up,
        received[0],
        received[1],
    )


def solution(mesh):
    in_specs = (
        P("ctx", "head"),
        P("head", None),
        P(None, "head"),
        P("ctx", "head"),
        P("ctx", "head"),
        P("ctx", "head"),
        P("ctx", "head"),
    )
    out_specs = (
        P("ctx", "head"),
        P("ctx", "head"),
        P("head", None),
        P(None, "head"),
        P("ctx", "head"),
        P("ctx", "head"),
    )
    return jax.shard_map(
        on_device, mesh=mesh, in_specs=in_specs, out_specs=out_specs, check_vma=False
    )
```
